32 devices in a mesh: row: 4 (over z), col: 8 (over y, x, core).
Axes of the slice: x: 2, y: 2, z: 4, core: 2. Of those that a mesh axis runs over, the one named last changes fastest.
Arguments:
- feats: bfloat16 [2048, 4096], P('row', 'col'), may hold values from -6 to 6
- prior_factor: bfloat16 [2048, 2048], P('row', 'col'), may hold values from -0.02 to 0.02, as said below
- ridge: float32 [1024], P('col'), may hold values from 0.5 to 2
Outputs:
- factor: float32 [2048, 1024], P('row', 'col')
The draws below stay inside these ranges and needn't reach their ends.
Inputs may be any that keep to these rules, and one draw needn't show every extreme that they name: `prior_factor`: entries are independent.
All inputs are finite; a program needn't handle non-finite values.
Results may differ from the reference program's by a relative error of at most 0.0003.
Values may be sent and summed in bfloat16 or wider, within the bound.
A program may use at most 128 MiB of HBM per device.

```python
import math
import jax
import jax.numpy as jnp
from jax import lax

EDGES = 4096
PRIOR = 2048
PANEL = 512
KCOLS = 1024
ROWS_DEV = 512
NROWS = 2048
N_ROW = 4


def draw_prior_factor(key, part):
    shape = (NROWS, PRIOR)
    values = jnp.clip(jax.random.normal(key, shape, jnp.float32) * 0.008, -0.0198, 0.0198)
    return values.astype(jnp.bfloat16)


def steps_of(key, extent, shards, low, top_value):
    def one(dim, blocks):
        heights = jax.random.uniform(jax.random.fold_in(jax.random.fold_in(key, 6), dim), (blocks,), jnp.float32, low / len(shards), top_value / len(shards))
        return jnp.repeat(jnp.exp(heights), extent[dim] // blocks).reshape((-1,) + (1,) * (len(extent) - dim - 1))

    loudness = one(*shards[0])
    for cut in shards[1:]:
        loudness = loudness * one(*cut)
    return loudness


def normal_values(stream_key, dims, spread, limit, shards=(), dtype=jnp.bfloat16):
    result = spread * jax.random.normal(stream_key, dims, jnp.float32)
    if shards:
        result = result * steps_of(stream_key, dims, shards, -0.22, 0.18)
    return jnp.clip(result, -limit, limit).astype(dtype)


def setup_inputs(seed: int = 0) -> dict:
    splits = jax.random.split(jax.random.key(seed), 4)
    return {
        "feats": normal_values(splits[0], (NROWS, EDGES), 1.0, 6.0, ((0, 4), (1, 8))),
        "prior_factor": draw_prior_factor(jax.random.fold_in(splits[3], 71), 0),
        "ridge": jnp.clip(jnp.exp(math.log(2.0) - 1.3862944 * jax.random.uniform(splits[2], (KCOLS,), jnp.float32) ** steps_of(splits[2], (KCOLS,), ((0, 8),), -0.2, 0.2)), 0.5, 2.0),
    }


def subject_rows(parts, groups, count):
    width = parts.shape[-1]
    return parts.reshape(groups, count, width).transpose(1, 0, 2).reshape(groups * count, width)

def panel_cholesky(block, panel):
    top = jnp.linalg.cholesky(block[:panel, :panel])
    lower_left = jax.scipy.linalg.solve_triangular(top, block[panel:, :panel].T, lower=True).T
    rest = block[panel:, panel:] - jnp.dot(lower_left, lower_left.T, precision=lax.Precision.HIGHEST)
    bottom = jnp.linalg.cholesky(rest)
    upper = jnp.concatenate([top, jnp.zeros((panel, block.shape[0] - panel), jnp.float32)], axis=1)
    lower = jnp.concatenate([lower_left, bottom], axis=1)
    return jnp.concatenate([upper, lower], axis=0)

def reference(feats, prior_factor, ridge):
    subj_feats = subject_rows(feats, N_ROW, ROWS_DEV)
    subj_prior = subject_rows(prior_factor, N_ROW, ROWS_DEV)
    gram = jnp.dot(subj_feats.astype(jnp.float32), subj_feats[:KCOLS].T.astype(jnp.float32), preferred_element_type=jnp.float32)
    update = jnp.dot(subj_prior.astype(jnp.float32), subj_prior[:KCOLS].T.astype(jnp.float32), preferred_element_type=jnp.float32)
    wide = subj_feats.astype(jnp.float32)
    squares = jnp.sum(wide * wide, axis=1)
    kernel = jnp.exp(-(squares[:, None] + squares[None, :KCOLS] - 2.0 * gram) / EDGES)
    subject = lax.broadcasted_iota(jnp.int32, (NROWS, KCOLS), 0)
    column = lax.broadcasted_iota(jnp.int32, (NROWS, KCOLS), 1)
    system = kernel + jnp.where(subject == column, ridge[None, :], jnp.zeros_like(kernel)) - update
    diag_factor = panel_cholesky(system[:KCOLS], PANEL)
    solved = jax.scipy.linalg.solve_triangular(diag_factor, system.T, lower=True).T
    return solved.reshape(ROWS_DEV, N_ROW, KCOLS).transpose(1, 0, 2).reshape(NROWS, KCOLS)
```

```python
import jax
import jax.numpy as jnp
from jax import lax
from jax.sharding import PartitionSpec as P
from jax.experimental import pallas as pl
from jax.experimental.pallas import tpu as pltpu

NB = 128
PB = 16


def split2(x):
    hi = x.astype(jnp.bfloat16)
    lo = (x - hi.astype(jnp.float32)).astype(jnp.bfloat16)
    return hi, lo


def dot3(a, b, b_dim=0):
    ah, al = split2(a)
    bh, bl = split2(b)
    return lax.dot_general(
        jnp.concatenate([ah, ah, al], axis=1),
        jnp.concatenate([bh, bl, bh], axis=b_dim),
        (((1,), (b_dim,)), ((), ())),
        preferred_element_type=jnp.float32,
    )


def spread(row, rows=8):
    return jnp.broadcast_to(row, (rows, row.shape[1]))


def factor_block(block):
    sub = lax.broadcasted_iota(jnp.int32, (8, NB), 0)
    sub2 = lax.broadcasted_iota(jnp.int32, (8, 2 * NB), 0)
    lane = lax.broadcasted_iota(jnp.int32, (NB, NB), 1)
    line = lax.broadcasted_iota(jnp.int32, (NB, NB), 0)
    trail = jnp.concatenate([block, (lane == line).astype(jnp.float32)], axis=1)
    nt = PB // 8
    done = []
    for p in range(NB // PB):
        base = p * PB
        panel = trail[:PB]
        rows = [panel[8 * t:8 * t + 8] for t in range(nt)]
        cols = [
            [
                jnp.broadcast_to(rows[t][:, base + j:base + j + 1], (8, NB)) if t >= j // 8 else None
                for t in range(nt)
            ]
            for j in range(PB)
        ]
        outs = [r for r in rows]
        for j in range(PB):
            tj, ij = divmod(j, 8)
            inv = lax.rsqrt(spread(cols[j][tj][ij:ij + 1]))
            col = [cols[j][t] * inv if t >= tj else None for t in range(nt)]
            prow = spread(rows[tj][ij:ij + 1]) * jnp.concatenate([inv, inv], axis=1)
            outs[tj] = jnp.where(sub2 == ij, prow, outs[tj])
            for k in range(j + 1, PB):
                tk, ik = divmod(k, 8)
                piv = spread(col[tk][ik:ik + 1])
                for t in range(tk, nt):
                    cols[k][t] = cols[k][t] - col[t] * piv
            for t in range(tj, nt):
                rows[t] = rows[t] - jnp.concatenate([col[t], col[t]], axis=1) * prow
        out = jnp.concatenate(outs, axis=0)
        done.append(out)
        if p < NB // PB - 1:
            oh, ol = split2(out)
            rhs = jnp.concatenate([oh, ol, oh], axis=0)
            left = jnp.transpose(out[:, :NB])
            lh, ll = split2(left[base + PB:])
            lhs = jnp.concatenate([lh, lh, ll], axis=1)
            prev = trail[PB:]
            trail = prev - jnp.dot(lhs, rhs, preferred_element_type=jnp.float32)
    full = jnp.concatenate(done, axis=0)
    return jnp.where(lane >= line, full[:, :NB], 0.0), full[:, NB:]


def chol_kernel(col_ref, b_hbm, s_hbm, o_ref, m_ref, t_ref, w_ref, sems):
    n = m_ref.shape[0]
    blocks = n // NB
    own = col_ref[0]
    grp = col_ref[1]
    groups = col_ref.shape[0] - 2
    heads = n // groups
    cb = pltpu.make_async_copy(b_hbm, m_ref, sems.at[0])
    cs = pltpu.make_async_copy(s_hbm, t_ref, sems.at[1])
    cb.start()
    cs.start()
    cb.wait()
    cs.wait()

    def step(k, carry):
        at = pl.ds(pl.multiple_of(k * NB, NB), NB)
        u, w = factor_block(m_ref[at, at])
        new = dot3(w, m_ref[at, :])
        m_ref[at, :] = new
        m_ref[at, at] = u
        x = dot3(t_ref[:, at], w, 1)
        t_ref[...] = t_ref[...] - dot3(x, new)

        @pl.when(k == own)
        def _():
            o_ref[heads:, :] = x
            line = lax.broadcasted_iota(jnp.int32, (NB, n), 0) + k * NB
            lane = lax.broadcasted_iota(jnp.int32, (NB, n), 1)
            mine = jnp.where(lane >= line, m_ref[at, :], 0.0)
            pick = (
                lax.broadcasted_iota(jnp.int32, (heads, n), 1)
                == lax.broadcasted_iota(jnp.int32, (heads, n), 0) * groups + grp
            ).astype(jnp.bfloat16)
            hi, lo = split2(mine)
            lo2 = (mine - hi.astype(jnp.float32) - lo.astype(jnp.float32)).astype(jnp.bfloat16)
            nt = (((1,), (1,)), ((), ()))
            o_ref[:heads, :] = sum(
                lax.dot_general(pick, v, nt, preferred_element_type=jnp.float32) for v in (hi, lo, lo2)
            )

        def update(j, c):
            aj = pl.ds(pl.multiple_of(j * NB, NB), NB)
            m_ref[aj, :] = m_ref[aj, :] - dot3(jnp.transpose(m_ref[at, aj]), m_ref[at, :])
            return c

        lax.fori_loop(k + 1, blocks, update, 0)
        return carry

    lax.fori_loop(0, blocks, step, 0)


def chol_solve(square, rest, own, grp, groups):
    n = square.shape[0]
    pos = jnp.stack([own, grp] + [jnp.int32(0)] * groups).astype(jnp.int32)
    return pl.pallas_call(
        chol_kernel,
        out_shape=jax.ShapeDtypeStruct((n // groups + rest.shape[0], NB), jnp.float32),
        in_specs=[
            pl.BlockSpec(memory_space=pltpu.SMEM),
            pl.BlockSpec(memory_space=pl.ANY),
            pl.BlockSpec(memory_space=pl.ANY),
        ],
        out_specs=pl.BlockSpec(memory_space=pltpu.VMEM),
        scratch_shapes=[
            pltpu.VMEM((n, n), jnp.float32),
            pltpu.VMEM(rest.shape, jnp.float32),
            pltpu.VMEM((NB, NB), jnp.float32),
            pltpu.SemaphoreType.DMA((2,)),
        ],
        compiler_params=pltpu.CompilerParams(vmem_limit_bytes=48 * 1024 * 1024),
    )(pos, square, rest)


EDGES = 4096


def subject_rows(parts, groups, count):
    width = parts.shape[-1]
    return parts.reshape(groups, count, width).transpose(1, 0, 2).reshape(groups * count, width)


def dealt(head, tail, lanes):
    width = head.shape[1]
    both = [head.reshape(lanes, -1, width), tail.reshape(lanes, -1, width)]
    return jnp.concatenate(both, axis=1).reshape(-1, width)


def body(feats, prior_factor, ridge):
    groups = lax.axis_size("row")
    lanes = lax.axis_size("col")
    row_pos = lax.axis_index("row")
    col_pos = lax.axis_index("col")
    cols_here = ridge.shape[0]
    total_cols = cols_here * lanes
    leading = total_cols // groups
    share = leading // lanes
    col_feats, col_prior = (
        lax.all_gather(feats[:leading], "row", axis=0, tiled=True),
        lax.all_gather(prior_factor[:leading], "row", axis=0, tiled=True),
    )
    col_feats = subject_rows(col_feats, groups, leading)
    col_prior = subject_rows(col_prior, groups, leading)
    first = row_pos * leading
    rows_feats = dealt(lax.dynamic_slice_in_dim(col_feats, first, leading), feats[leading:], lanes)
    rows_prior = dealt(lax.dynamic_slice_in_dim(col_prior, first, leading), prior_factor[leading:], lanes)
    subject = dealt(
        first + lax.broadcasted_iota(jnp.int32, (leading, 1), 0),
        jnp.full((feats.shape[0] - leading, 1), -1, jnp.int32),
        lanes,
    )
    col_start = col_pos * cols_here
    column = lax.broadcasted_iota(jnp.int32, (1, total_cols), 1)
    own_ridge = lax.dynamic_update_slice(jnp.zeros((total_cols,), jnp.float32), ridge, (col_start,))
    wide_rows = rows_feats.astype(jnp.float32)
    wide_cols = col_feats.astype(jnp.float32)
    gram = jnp.dot(rows_feats, col_feats.T, preferred_element_type=jnp.float32)
    dist = (
        jnp.sum(wide_rows * wide_rows, axis=1)[:, None]
        + jnp.sum(wide_cols * wide_cols, axis=1)[None, :]
        - 2.0 * gram
    )
    update = jnp.dot(rows_prior, col_prior.T, preferred_element_type=jnp.float32)
    update = update - jnp.where(subject == column, own_ridge[None, :], 0.0)
    sums = lax.psum_scatter(
        jnp.concatenate([dist, update], axis=1), "col", scatter_dimension=0, tiled=True
    )
    system = jnp.exp(-sums[:, :total_cols] / EDGES) - sums[:, total_cols:]
    square = lax.all_gather(system[:share], ("row", "col"), axis=0, tiled=True)
    rest = lax.all_gather(system[share:], "col", axis=0, tiled=True)
    out = chol_solve(square, rest, col_start // NB, row_pos, groups)
    if cols_here < NB:
        out = lax.dynamic_slice_in_dim(out, col_start % NB, cols_here, 1)
    return out


def solution(mesh):
    return jax.shard_map(
        body,
        mesh=mesh,
        in_specs=(P("row", "col"), P("row", "col"), P("col")),
        out_specs=P("row", "col"),
        check_vma=False,
    )
```

```python
import jax
import jax.numpy as jnp
from jax import lax
from jax.sharding import PartitionSpec as P
from jax.experimental import pallas as pl
from jax.experimental.pallas import tpu as pltpu

NB = 128
PB = 16


def split2(x):
    hi = x.astype(jnp.bfloat16)
    lo = (x - hi.astype(jnp.float32)).astype(jnp.bfloat16)
    return hi, lo


def dot3(a, b, b_dim=0):
    ah, al = split2(a)
    bh, bl = split2(b)
    return lax.dot_general(
        jnp.concatenate([ah, ah, al], axis=1),
        jnp.concatenate([bh, bl, bh], axis=b_dim),
        (((1,), (b_dim,)), ((), ())),
        preferred_element_type=jnp.float32,
    )


def spread(row, rows=8):
    return jnp.broadcast_to(row, (rows, row.shape[1]))


def factor_block(block):
    sub = lax.broadcasted_iota(jnp.int32, (8, NB), 0)
    sub2 = lax.broadcasted_iota(jnp.int32, (8, 2 * NB), 0)
    lane = lax.broadcasted_iota(jnp.int32, (NB, NB), 1)
    line = lax.broadcasted_iota(jnp.int32, (NB, NB), 0)
    trail = jnp.concatenate([block, (lane == line).astype(jnp.float32)], axis=1)
    nt = PB // 8
    done = []
    for p in range(NB // PB):
        base = p * PB
        panel = trail[:PB]
        rows = [panel[8 * t:8 * t + 8] for t in range(nt)]
        cols = [
            [
                jnp.broadcast_to(rows[t][:, base + j:base + j + 1], (8, NB)) if t >= j // 8 else None
                for t in range(nt)
            ]
            for j in range(PB)
        ]
        outs = [r for r in rows]
        for j in range(PB):
            tj, ij = divmod(j, 8)
            inv = lax.rsqrt(spread(cols[j][tj][ij:ij + 1]))
            col = [cols[j][t] * inv if t >= tj else None for t in range(nt)]
            prow = spread(rows[tj][ij:ij + 1]) * jnp.concatenate([inv, inv], axis=1)
            outs[tj] = jnp.where(sub2 == ij, prow, outs[tj])
            for k in range(j + 1, PB):
                tk, ik = divmod(k, 8)
                piv = spread(col[tk][ik:ik + 1])
                for t in range(tk, nt):
                    cols[k][t] = cols[k][t] - col[t] * piv
            for t in range(tj, nt):
                rows[t] = rows[t] - jnp.concatenate([col[t], col[t]], axis=1) * prow
        out = jnp.concatenate(outs, axis=0)
        done.append(out)
        if p < NB // PB - 1:
            oh, ol = split2(out)
            rhs = jnp.concatenate([oh, ol, oh], axis=0)
            left = jnp.transpose(out[:, :NB])
            lh, ll = split2(left[base + PB:])
            lhs = jnp.concatenate([lh, lh, ll], axis=1)
            prev = trail[PB:]
            trail = prev - jnp.dot(lhs, rhs, preferred_element_type=jnp.float32)
    full = jnp.concatenate(done, axis=0)
    return jnp.where(lane >= line, full[:, :NB], 0.0), full[:, NB:]


def chol_kernel(col_ref, b_hbm, s_hbm, o_ref, m_ref, t_ref, w_ref, sems):
    n = m_ref.shape[0]
    blocks = n // NB
    own = col_ref[0]
    grp = col_ref[1]
    groups = col_ref.shape[0] - 2
    heads = n // groups
    cb = pltpu.make_async_copy(b_hbm, m_ref, sems.at[0])
    cs = pltpu.make_async_copy(s_hbm, t_ref, sems.at[1])
    cb.start()
    cs.start()
    cb.wait()
    cs.wait()

    def step(k, carry):
        at = pl.ds(pl.multiple_of(k * NB, NB), NB)
        u, w = factor_block(m_ref[at, at])
        new = dot3(w, m_ref[at, :])
        m_ref[at, :] = new
        m_ref[at, at] = u
        x = dot3(t_ref[:, at], w, 1)
        t_ref[...] = t_ref[...] - dot3(x, new)

        @pl.when(k == own)
        def _():
            o_ref[heads:, :] = x
            line = lax.broadcasted_iota(jnp.int32, (NB, n), 0) + k * NB
            lane = lax.broadcasted_iota(jnp.int32, (NB, n), 1)
            mine = jnp.where(lane >= line, m_ref[at, :], 0.0)
            pick = (
                lax.broadcasted_iota(jnp.int32, (heads, n), 1)
                == lax.broadcasted_iota(jnp.int32, (heads, n), 0) * groups + grp
            ).astype(jnp.bfloat16)
            hi, lo = split2(mine)
            lo2 = (mine - hi.astype(jnp.float32) - lo.astype(jnp.float32)).astype(jnp.bfloat16)
            nt = (((1,), (1,)), ((), ()))
            o_ref[:heads, :] = sum(
                lax.dot_general(pick, v, nt, preferred_element_type=jnp.float32) for v in (hi, lo, lo2)
            )

        def update(j, c):
            aj = pl.ds(pl.multiple_of(j * NB, NB), NB)
            m_ref[aj, :] = m_ref[aj, :] - dot3(jnp.transpose(m_ref[at, aj]), m_ref[at, :])
            return c

        lax.fori_loop(k + 1, blocks, update, 0)
        return carry

    lax.fori_loop(0, blocks, step, 0)


def chol_solve(square, rest, own, grp, groups):
    n = square.shape[0]
    pos = jnp.stack([own, grp] + [jnp.int32(0)] * groups).astype(jnp.int32)
    return pl.pallas_call(
        chol_kernel,
        out_shape=jax.ShapeDtypeStruct((n // groups + rest.shape[0], NB), jnp.float32),
        in_specs=[
            pl.BlockSpec(memory_space=pltpu.SMEM),
            pl.BlockSpec(memory_space=pl.ANY),
            pl.BlockSpec(memory_space=pl.ANY),
        ],
        out_specs=pl.BlockSpec(memory_space=pltpu.VMEM),
        scratch_shapes=[
            pltpu.VMEM((n, n), jnp.float32),
            pltpu.VMEM(rest.shape, jnp.float32),
            pltpu.VMEM((NB, NB), jnp.float32),
            pltpu.SemaphoreType.DMA((2,)),
        ],
        compiler_params=pltpu.CompilerParams(vmem_limit_bytes=48 * 1024 * 1024),
    )(pos, square, rest)


EDGES = 4096
MESH = pl.DeviceIdType.MESH


def exchange_kernel(parts_ref, sq_ref, rs_ref, got1, acc, got2, send1, recv1, send2, recv2, sends, arrive):
    groups, lanes = sq_ref.shape[:2]
    share, width = sq_ref.shape[2:]
    i = lax.axis_index("row")
    c = lax.axis_index("col")
    core, x, y = lax.rem(c, 2), lax.rem(c // 2, 2), c // 4
    sib = c + 1 - 2 * core
    xn = c + 2 - 4 * x
    yn = c + 4 - 8 * y
    dg = xn + 4 - 8 * y
    planes = [lax.rem(i + d, groups) for d in range(groups)]
    barrier = pltpu.get_barrier_semaphore()
    for col in (sib, xn, yn, dg):
        pl.semaphore_signal(barrier, inc=1, device_id=(i, col), device_id_type=MESH)
    for z in planes[1:]:
        pl.semaphore_signal(barrier, inc=1, device_id=(z, c), device_id_type=MESH)
    pl.semaphore_wait(barrier, 3 + groups)

    def remote(src, dst, s, r, target):
        copy = pltpu.make_async_remote_copy(
            src_ref=src, dst_ref=dst, send_sem=s, recv_sem=r, device_id=target, device_id_type=MESH
        )
        copy.start()
        return copy

    order = [dg // 2, xn // 2, yn // 2, c // 2]
    pair = [
        remote(parts_ref.at[q, 1 - core], got1.at[n], send1.at[n], recv1.at[n], (i, sib))
        for n, q in enumerate(order)
    ]
    across = []
    for n, q in enumerate(order):
        pair[n].wait_recv()
        acc[n] = parts_ref[q, core] + got1[n]
        if n < 3:
            across.append(
                remote(acc.at[n], got2.at[n], send2.at[n], recv2.at[n], (i, (dg, xn, yn)[n]))
            )
    for copy in across:
        copy.wait_recv()
    total = acc[3] + got2[0] + got2[1] + got2[2]
    system = jnp.exp(-total[:, :width] / EDGES) - total[:, width:]
    sq_ref[i, c] = system[:share]
    rs_ref[c] = system[share:]

    started = []

    def pass_on(z, col, target):
        n = len(started)
        started.append(
            remote(sq_ref.at[z, col], sq_ref.at[z, col], sends.at[n], arrive.at[z * lanes + col], target)
        )

    def pass_rest(col, target):
        n = len(started)
        started.append(
            remote(rs_ref.at[col], rs_ref.at[col], sends.at[n], arrive.at[groups * lanes + col], target)
        )

    def await_block(z, col):
        pltpu.make_async_copy(sq_ref.at[z, col], sq_ref.at[z, col], arrive.at[z * lanes + col]).wait()

    def await_rest(col):
        pltpu.make_async_copy(rs_ref.at[col], rs_ref.at[col], arrive.at[groups * lanes + col]).wait()

    for z in planes[1:]:
        pass_on(i, c, (z, c))
    for z in planes:
        if z is not planes[0]:
            await_block(z, c)
        pass_on(z, c, (i, xn))
        pass_on(z, c, (i, yn))
        pass_on(z, c, (i, sib))
        if z is planes[0]:
            for col in (xn, yn, sib):
                pass_rest(c, (i, col))
    for n, z in enumerate(planes):
        await_block(z, xn)
        if n < groups // 2:
            pass_on(z, xn, (i, yn))
        pass_on(z, xn, (i, sib))
        await_block(z, yn)
        if n >= groups // 2:
            pass_on(z, yn, (i, xn))
        pass_on(z, yn, (i, sib))
        if n == 0:
            await_rest(xn)
            pass_rest(xn, (i, yn))
            pass_rest(xn, (i, sib))
            await_rest(yn)
            pass_rest(yn, (i, sib))
    for n, z in enumerate(planes):
        await_block(z, dg)
        pass_on(z, dg, (i, sib))
        if n == 0:
            await_rest(dg)
            pass_rest(dg, (i, sib))
    other = [sib + d for d in (0, xn - c, yn - c, dg - c)]
    for col in other:
        for z in planes:
            await_block(z, col)
        await_rest(col)
    for copy in pair + across + started:
        copy.wait_send()


def exchange(parts, groups, lanes, share):
    rows, wide = parts.shape
    each = rows // lanes
    width = wide // 2
    f32 = jnp.float32
    dma = pltpu.SemaphoreType.DMA
    vmem = pl.BlockSpec(memory_space=pltpu.VMEM)
    square, rest = pl.pallas_call(
        exchange_kernel,
        out_shape=(
            jax.ShapeDtypeStruct((groups, lanes, share, width), f32),
            jax.ShapeDtypeStruct((lanes, each - share, width), f32),
        ),
        in_specs=[vmem],
        out_specs=(vmem, vmem),
        scratch_shapes=[
            pltpu.VMEM((4, each, wide), f32),
            pltpu.VMEM((4, each, wide), f32),
            pltpu.VMEM((3, each, wide), f32),
            dma((4,)),
            dma((4,)),
            dma((3,)),
            dma((3,)),
            dma((64,)),
            dma((groups * lanes + lanes,)),
        ],
        compiler_params=pltpu.CompilerParams(
            collective_id=1, has_side_effects=True, vmem_limit_bytes=40 * 1024 * 1024
        ),
    )(parts.reshape(lanes // 2, 2, each, wide))
    return square.reshape(-1, width), rest.reshape(-1, width)

def subject_rows(parts, groups, count):
    width = parts.shape[-1]
    return parts.reshape(groups, count, width).transpose(1, 0, 2).reshape(groups * count, width)


def dealt(head, tail, lanes):
    width = head.shape[1]
    both = [head.reshape(lanes, -1, width), tail.reshape(lanes, -1, width)]
    return jnp.concatenate(both, axis=1).reshape(-1, width)


def body(feats, prior_factor, ridge):
    groups = lax.axis_size("row")
    lanes = lax.axis_size("col")
    row_pos = lax.axis_index("row")
    col_pos = lax.axis_index("col")
    cols_here = ridge.shape[0]
    total_cols = cols_here * lanes
    leading = total_cols // groups
    share = leading // lanes
    col_feats, col_prior = (
        lax.all_gather(feats[:leading], "row", axis=0, tiled=True),
        lax.all_gather(prior_factor[:leading], "row", axis=0, tiled=True),
    )
    col_feats = subject_rows(col_feats, groups, leading)
    col_prior = subject_rows(col_prior, groups, leading)
    first = row_pos * leading
    rows_feats = dealt(lax.dynamic_slice_in_dim(col_feats, first, leading), feats[leading:], lanes)
    rows_prior = dealt(lax.dynamic_slice_in_dim(col_prior, first, leading), prior_factor[leading:], lanes)
    subject = dealt(
        first + lax.broadcasted_iota(jnp.int32, (leading, 1), 0),
        jnp.full((feats.shape[0] - leading, 1), -1, jnp.int32),
        lanes,
    )
    col_start = col_pos * cols_here
    column = lax.broadcasted_iota(jnp.int32, (1, total_cols), 1)
    own_ridge = lax.dynamic_update_slice(jnp.zeros((total_cols,), jnp.float32), ridge, (col_start,))
    wide_rows = rows_feats.astype(jnp.float32)
    wide_cols = col_feats.astype(jnp.float32)
    gram = jnp.dot(rows_feats, col_feats.T, preferred_element_type=jnp.float32)
    dist = (
        jnp.sum(wide_rows * wide_rows, axis=1)[:, None]
        + jnp.sum(wide_cols * wide_cols, axis=1)[None, :]
        - 2.0 * gram
    )
    update = jnp.dot(rows_prior, col_prior.T, preferred_element_type=jnp.float32)
    update = update - jnp.where(subject == column, own_ridge[None, :], 0.0)
    parts = jnp.concatenate([dist, update], axis=1)
    if (groups, lanes) == (4, 8):
        square, rest = exchange(parts, groups, lanes, share)
    else:
        sums = lax.psum_scatter(
            parts, "col", scatter_dimension=0, tiled=True
        )
        system = jnp.exp(-sums[:, :total_cols] / EDGES) - sums[:, total_cols:]
        square = lax.all_gather(system[:share], ("row", "col"), axis=0, tiled=True)
        rest = lax.all_gather(system[share:], "col", axis=0, tiled=True)
    out = chol_solve(square, rest, col_start // NB, row_pos, groups)
    if cols_here < NB:
        out = lax.dynamic_slice_in_dim(out, col_start % NB, cols_here, 1)
    return out


def solution(mesh):
    return jax.shard_map(
        body,
        mesh=mesh,
        in_specs=(P("row", "col"), P("row", "col"), P("col")),
        out_specs=P("row", "col"),
        check_vma=False,
    )
```

```python
import functools
import jax
import jax.numpy as jnp
from jax import lax
from jax.sharding import PartitionSpec as P
from jax.experimental import pallas as pl
from jax.experimental.pallas import tpu as pltpu

NB = 128
PB = 32
TILE = 256
STOPS = (1, 2)


def split2(x):
    hi = x.astype(jnp.bfloat16)
    lo = (x - hi.astype(jnp.float32)).astype(jnp.bfloat16)
    return hi, lo


def dot3(a, b, b_dim=0):
    ah, al = split2(a)
    bh, bl = split2(b)
    return lax.dot_general(
        jnp.concatenate([ah, ah, al], axis=1),
        jnp.concatenate([bh, bl, bh], axis=b_dim),
        (((1,), (b_dim,)), ((), ())),
        preferred_element_type=jnp.float32,
    )


def spread(row, rows=8):
    return jnp.broadcast_to(row, (rows, row.shape[1]))


def factor_block(block):
    sub = lax.broadcasted_iota(jnp.int32, (8, NB), 0)
    sub2 = lax.broadcasted_iota(jnp.int32, (8, 2 * NB), 0)
    lane = lax.broadcasted_iota(jnp.int32, (NB, NB), 1)
    line = lax.broadcasted_iota(jnp.int32, (NB, NB), 0)
    trail = jnp.concatenate([block, (lane == line).astype(jnp.float32)], axis=1)
    nt = PB // 8
    done = []
    for p in range(NB // PB):
        base = p * PB
        panel = trail[:PB]
        rows = [panel[8 * t:8 * t + 8] for t in range(nt)]
        cols = [
            [
                jnp.broadcast_to(rows[t][:, base + j:base + j + 1], (8, NB)) if t >= j // 8 else None
                for t in range(nt)
            ]
            for j in range(PB)
        ]
        outs = [r for r in rows]
        for j in range(PB):
            tj, ij = divmod(j, 8)
            inv = lax.rsqrt(spread(cols[j][tj][ij:ij + 1]))
            col = [cols[j][t] * inv if t >= tj else None for t in range(nt)]
            prow = spread(rows[tj][ij:ij + 1]) * jnp.concatenate([inv, inv], axis=1)
            outs[tj] = jnp.where(sub2 == ij, prow, outs[tj])
            for k in range(j + 1, PB):
                tk, ik = divmod(k, 8)
                piv = spread(col[tk][ik:ik + 1])
                for t in range(tk, nt):
                    cols[k][t] = cols[k][t] - col[t] * piv
            for t in range(tj, nt):
                rows[t] = rows[t] - jnp.concatenate([col[t], col[t]], axis=1) * prow
        out = jnp.concatenate(outs, axis=0)
        done.append(out)
        if p < NB // PB - 1:
            oh, ol = split2(out)
            rhs = jnp.concatenate([oh, ol, oh], axis=0)
            left = jnp.transpose(out[:, :NB])
            lh, ll = split2(left[base + PB:])
            lhs = jnp.concatenate([lh, lh, ll], axis=1)
            prev = trail[PB:]
            trail = prev - jnp.dot(lhs, rhs, preferred_element_type=jnp.float32)
    full = jnp.concatenate(done, axis=0)
    return jnp.where(lane >= line, full[:, :NB], 0.0), full[:, NB:]


def chol_kernel(col_ref, b_hbm, s_hbm, o_ref, m_ref, t_ref, l_ref, r_ref, x_ref, sems):
    n = m_ref.shape[0]
    blocks = n // NB
    own = col_ref[0]
    grp = col_ref[1]
    groups = col_ref.shape[0] - 2
    heads = n // groups
    cb = pltpu.make_async_copy(b_hbm, m_ref, sems.at[0])
    cs = pltpu.make_async_copy(s_hbm, t_ref, sems.at[1])
    cb.start()
    cs.start()
    cb.wait()
    cs.wait()

    def split_rows(v):
        hi, lo = split2(v)
        return jnp.concatenate([hi, lo, hi], axis=0)

    def split_cols(v):
        hi, lo = split2(v)
        return jnp.concatenate([hi, hi, lo], axis=1)

    def step(k, carry, low):
        at = pl.ds(pl.multiple_of(k * NB, NB), NB)
        diag = m_ref[at, at]
        for tile in range(low, n, TILE):
            right = r_ref[:, tile:tile + TILE]
            m_ref[low:tile + TILE, tile:tile + TILE] -= jnp.dot(
                l_ref[low:tile + TILE, :], right, preferred_element_type=jnp.float32
            )
            t_ref[:, tile:tile + TILE] -= jnp.dot(x_ref[...], right, preferred_element_type=jnp.float32)
        u, w = factor_block(diag)
        new = dot3(w, m_ref[at, low:])
        m_ref[at, low:] = new
        m_ref[at, at] = u
        x = dot3(t_ref[:, at], w, 1)
        r_ref[:, low:] = split_rows(new)
        x_ref[...] = split_cols(x)

        @pl.when(k == own)
        def _():
            o_ref[heads:, :] = x
            line = lax.broadcasted_iota(jnp.int32, (NB, n - low), 0) + k * NB
            lane = lax.broadcasted_iota(jnp.int32, (NB, n - low), 1) + low
            mine = jnp.where(lane >= line, m_ref[at, low:], 0.0)
            pick = (
                lax.broadcasted_iota(jnp.int32, (heads, n - low), 1) + low
                == lax.broadcasted_iota(jnp.int32, (heads, n - low), 0) * groups + grp
            ).astype(jnp.bfloat16)
            hi, lo = split2(mine)
            lo2 = (mine - hi.astype(jnp.float32) - lo.astype(jnp.float32)).astype(jnp.bfloat16)
            nt = (((1,), (1,)), ((), ()))
            o_ref[:heads, :] = sum(
                lax.dot_general(pick, v, nt, preferred_element_type=jnp.float32) for v in (hi, lo, lo2)
            )

        @pl.when(k + 1 < blocks)
        def _():
            nxt = pl.ds(pl.multiple_of((k + 1) * NB, NB), NB)
            m_ref[nxt, low:] -= jnp.dot(
                split_cols(jnp.transpose(m_ref[at, nxt])), r_ref[:, low:], preferred_element_type=jnp.float32
            )
            lane = lax.broadcasted_iota(jnp.int32, (NB, n - low), 1) + low
            later = jnp.where(lane >= (k + 2) * NB, new, 0.0)
            l_ref[low:, :] = split_cols(jnp.transpose(later))

        return carry

    r_ref[...] = jnp.zeros_like(r_ref)
    l_ref[...] = jnp.zeros_like(l_ref)
    x_ref[...] = jnp.zeros_like(x_ref)
    first = 0
    for last in STOPS:
        stop = blocks * last // STOPS[-1]
        lax.fori_loop(first, stop, functools.partial(step, low=first * NB), 0)
        first = stop


def chol_solve(square, rest, own, grp, groups):
    n = square.shape[0]
    pos = jnp.stack([own, grp] + [jnp.int32(0)] * groups).astype(jnp.int32)
    return pl.pallas_call(
        chol_kernel,
        out_shape=jax.ShapeDtypeStruct((n // groups + rest.shape[0], NB), jnp.float32),
        in_specs=[
            pl.BlockSpec(memory_space=pltpu.SMEM),
            pl.BlockSpec(memory_space=pl.ANY),
            pl.BlockSpec(memory_space=pl.ANY),
        ],
        out_specs=pl.BlockSpec(memory_space=pltpu.VMEM),
        scratch_shapes=[
            pltpu.VMEM((n, n), jnp.float32),
            pltpu.VMEM(rest.shape, jnp.float32),
            pltpu.VMEM((n, 3 * NB), jnp.bfloat16),
            pltpu.VMEM((3 * NB, n), jnp.bfloat16),
            pltpu.VMEM((rest.shape[0], 3 * NB), jnp.bfloat16),
            pltpu.SemaphoreType.DMA((2,)),
        ],
        compiler_params=pltpu.CompilerParams(vmem_limit_bytes=48 * 1024 * 1024),
    )(pos, square, rest)


EDGES = 4096
MESH = pl.DeviceIdType.MESH


def exchange_kernel(feats_ref, prior_ref, ridge_ref, sq_ref, rs_ref, gf, gp, ff, fp, parts_ref, sendf, recvf,
                    sendp, recvp, got1, acc, got2, send1, recv1, send2, recv2, sends, arrive):
    groups, lanes = sq_ref.shape[:2]
    share, width = sq_ref.shape[2:]
    i = lax.axis_index("row")
    c = lax.axis_index("col")
    core, x, y = lax.rem(c, 2), lax.rem(c // 2, 2), c // 4
    sib = c + 1 - 2 * core
    xn = c + 2 - 4 * x
    yn = c + 4 - 8 * y
    dg = xn + 4 - 8 * y
    planes = [lax.rem(i + d, groups) for d in range(groups)]
    barrier = pltpu.get_barrier_semaphore()
    for col in (sib, xn, yn, dg):
        pl.semaphore_signal(barrier, inc=1, device_id=(i, col), device_id_type=MESH)
    for z in planes[1:]:
        pl.semaphore_signal(barrier, inc=1, device_id=(z, c), device_id_type=MESH)
    pl.semaphore_wait(barrier, 3 + groups)

    def remote(src, dst, s, r, target):
        copy = pltpu.make_async_remote_copy(
            src_ref=src, dst_ref=dst, send_sem=s, recv_sem=r, device_id=target, device_id_type=MESH
        )
        copy.start()
        return copy

    heads = lanes * share
    early = []
    for d, z in enumerate(planes[1:]):
        early.append(remote(feats_ref.at[:heads], gf.at[i], sendf.at[d], recvf.at[i], (z, c)))
    for d, z in enumerate(planes[1:]):
        early.append(remote(prior_ref.at[:heads], gp.at[i], sendp.at[d], recvp.at[i], (z, c)))

    def place(z, value):
        pick = lax.broadcasted_iota(jnp.int32, (width, heads), 0) == (
            lax.broadcasted_iota(jnp.int32, (width, heads), 1) * groups + z
        )
        return jnp.dot(pick.astype(jnp.bfloat16), value, preferred_element_type=jnp.float32)

    def interleave(own_ref, got, to, sem):
        to[...] = place(i, own_ref[:heads, :])
        for z in planes[1:]:
            pltpu.make_async_copy(got.at[z], got.at[z], sem.at[z]).wait()
            to[...] += place(z, got[z])

    nt = (((1,), (1,)), ((), ()))

    def dot_nt(a, b):
        return lax.dot_general(a, b, nt, preferred_element_type=jnp.float32)

    mine = pl.ds(pl.multiple_of(i * heads, heads), heads)
    interleave(feats_ref, gf, ff, recvf)
    wide = ff[...]
    cols = wide.astype(jnp.bfloat16)
    hi, lo = split2(wide * wide)
    ones = jnp.ones((8, wide.shape[1]), jnp.bfloat16)
    col_sq = (dot_nt(ones, hi) + dot_nt(ones, lo))[:1]
    lead = ff[mine, :]
    tail = feats_ref[heads:, :]
    for n, rows in enumerate((lead.astype(jnp.bfloat16), tail)):
        own = rows.astype(jnp.float32)
        dist = jnp.sum(own * own, axis=1, keepdims=True) + col_sq - 2.0 * dot_nt(rows, cols)
        each = rows.shape[0] // lanes
        for k in range(lanes):
            parts_ref[k // 2, k % 2, n * share:n * share + each, :width] = dist[k * each:k * each + each]
    interleave(prior_ref, gp, fp, recvp)
    cols = fp[...].astype(jnp.bfloat16)
    line = lax.broadcasted_iota(jnp.int32, (heads, width), 0) + i * heads
    lane = lax.broadcasted_iota(jnp.int32, (heads, width), 1)
    first = c * (width // lanes)
    here = (lane == line) & (lane >= first) & (lane < first + width // lanes)
    ridge = jnp.where(here, jnp.concatenate([ridge_ref[...]] * lanes, axis=1), 0.0)
    for n, rows in enumerate((fp[mine, :].astype(jnp.bfloat16), prior_ref[heads:, :])):
        update = dot_nt(rows, cols)
        if n == 0:
            update = update - ridge
        each = rows.shape[0] // lanes
        for k in range(lanes):
            parts_ref[k // 2, k % 2, n * share:n * share + each, width:] = update[k * each:k * each + each]

    order = [dg // 2, xn // 2, yn // 2, c // 2]
    pair = [
        remote(parts_ref.at[q, 1 - core], got1.at[n], send1.at[n], recv1.at[n], (i, sib))
        for n, q in enumerate(order)
    ]
    across = []
    for n, q in enumerate(order):
        pair[n].wait_recv()
        acc[n] = parts_ref[q, core] + got1[n]
        if n < 3:
            across.append(
                remote(acc.at[n], got2.at[n], send2.at[n], recv2.at[n], (i, (dg, xn, yn)[n]))
            )
    for copy in across:
        copy.wait_recv()
    total = acc[3] + got2[0] + got2[1] + got2[2]
    system = jnp.exp(-total[:, :width] / EDGES) - total[:, width:]
    sq_ref[i, c] = system[:share]
    rs_ref[c] = system[share:]

    started = []

    def pass_on(z, col, target):
        n = len(started)
        started.append(
            remote(sq_ref.at[z, col], sq_ref.at[z, col], sends.at[n], arrive.at[z * lanes + col], target)
        )

    def pass_rest(col, target):
        n = len(started)
        started.append(
            remote(rs_ref.at[col], rs_ref.at[col], sends.at[n], arrive.at[groups * lanes + col], target)
        )

    def await_block(z, col):
        pltpu.make_async_copy(sq_ref.at[z, col], sq_ref.at[z, col], arrive.at[z * lanes + col]).wait()

    def await_rest(col):
        pltpu.make_async_copy(rs_ref.at[col], rs_ref.at[col], arrive.at[groups * lanes + col]).wait()

    for z in planes[1:]:
        pass_on(i, c, (z, c))
    for z in planes:
        if z is not planes[0]:
            await_block(z, c)
        pass_on(z, c, (i, xn))
        pass_on(z, c, (i, yn))
        pass_on(z, c, (i, sib))
        if z is planes[0]:
            for col in (xn, yn, sib):
                pass_rest(c, (i, col))
    for n, z in enumerate(planes):
        await_block(z, xn)
        if n < groups // 2:
            pass_on(z, xn, (i, yn))
        pass_on(z, xn, (i, sib))
        await_block(z, yn)
        if n >= groups // 2:
            pass_on(z, yn, (i, xn))
        pass_on(z, yn, (i, sib))
        if n == 0:
            await_rest(xn)
            pass_rest(xn, (i, yn))
            pass_rest(xn, (i, sib))
            await_rest(yn)
            pass_rest(yn, (i, sib))
    for n, z in enumerate(planes):
        await_block(z, dg)
        pass_on(z, dg, (i, sib))
        if n == 0:
            await_rest(dg)
            pass_rest(dg, (i, sib))
    other = [sib + d for d in (0, xn - c, yn - c, dg - c)]
    for col in other:
        for z in planes:
            await_block(z, col)
        await_rest(col)
    for copy in early + pair + across + started:
        copy.wait_send()


def exchange(feats, prior, ridge, groups, lanes, share):
    width = ridge.shape[0] * lanes
    each = feats.shape[0] // lanes
    heads = lanes * share
    wide = 2 * width
    f32 = jnp.float32
    dma = pltpu.SemaphoreType.DMA
    vmem = pl.BlockSpec(memory_space=pltpu.VMEM)
    square, rest = pl.pallas_call(
        exchange_kernel,
        out_shape=(
            jax.ShapeDtypeStruct((groups, lanes, share, width), f32),
            jax.ShapeDtypeStruct((lanes, each - share, width), f32),
        ),
        in_specs=[vmem, vmem, vmem],
        out_specs=(vmem, vmem),
        scratch_shapes=[
            pltpu.VMEM((groups, heads, feats.shape[1]), feats.dtype),
            pltpu.VMEM((groups, heads, prior.shape[1]), prior.dtype),
            pltpu.VMEM((width, feats.shape[1]), f32),
            pltpu.VMEM((width, prior.shape[1]), f32),
            pltpu.VMEM((lanes // 2, 2, each, wide), f32),
            dma((groups - 1,)),
            dma((groups,)),
            dma((groups - 1,)),
            dma((groups,)),
            pltpu.VMEM((4, each, wide), f32),
            pltpu.VMEM((4, each, wide), f32),
            pltpu.VMEM((3, each, wide), f32),
            dma((4,)),
            dma((4,)),
            dma((3,)),
            dma((3,)),
            dma((64,)),
            dma((groups * lanes + lanes,)),
        ],
        compiler_params=pltpu.CompilerParams(
            collective_id=1, has_side_effects=True, vmem_limit_bytes=56 * 1024 * 1024
        ),
    )(feats, prior, ridge[None, :])
    return square.reshape(-1, width), rest.reshape(-1, width)

def subject_rows(parts, groups, count):
    width = parts.shape[-1]
    return parts.reshape(groups, count, width).transpose(1, 0, 2).reshape(groups * count, width)


def dealt(head, tail, lanes):
    width = head.shape[1]
    both = [head.reshape(lanes, -1, width), tail.reshape(lanes, -1, width)]
    return jnp.concatenate(both, axis=1).reshape(-1, width)


def gathered(feats, prior_factor, ridge, groups, lanes, share):
    row_pos = lax.axis_index("row")
    col_pos = lax.axis_index("col")
    cols_here = ridge.shape[0]
    total_cols = cols_here * lanes
    leading = share * lanes
    col_feats, col_prior = (
        lax.all_gather(feats[:leading], "row", axis=0, tiled=True),
        lax.all_gather(prior_factor[:leading], "row", axis=0, tiled=True),
    )
    col_feats = subject_rows(col_feats, groups, leading)
    col_prior = subject_rows(col_prior, groups, leading)
    first = row_pos * leading
    rows_feats = dealt(lax.dynamic_slice_in_dim(col_feats, first, leading), feats[leading:], lanes)
    rows_prior = dealt(lax.dynamic_slice_in_dim(col_prior, first, leading), prior_factor[leading:], lanes)
    subject = dealt(
        first + lax.broadcasted_iota(jnp.int32, (leading, 1), 0),
        jnp.full((feats.shape[0] - leading, 1), -1, jnp.int32),
        lanes,
    )
    col_start = col_pos * cols_here
    column = lax.broadcasted_iota(jnp.int32, (1, total_cols), 1)
    own_ridge = lax.dynamic_update_slice(jnp.zeros((total_cols,), jnp.float32), ridge, (col_start,))
    wide_rows = rows_feats.astype(jnp.float32)
    wide_cols = col_feats.astype(jnp.float32)
    gram = jnp.dot(rows_feats, col_feats.T, preferred_element_type=jnp.float32)
    dist = (
        jnp.sum(wide_rows * wide_rows, axis=1)[:, None]
        + jnp.sum(wide_cols * wide_cols, axis=1)[None, :]
        - 2.0 * gram
    )
    update = jnp.dot(rows_prior, col_prior.T, preferred_element_type=jnp.float32)
    update = update - jnp.where(subject == column, own_ridge[None, :], 0.0)
    sums = lax.psum_scatter(
        jnp.concatenate([dist, update], axis=1), "col", scatter_dimension=0, tiled=True
    )
    system = jnp.exp(-sums[:, :total_cols] / EDGES) - sums[:, total_cols:]
    square = lax.all_gather(system[:share], ("row", "col"), axis=0, tiled=True)
    rest = lax.all_gather(system[share:], "col", axis=0, tiled=True)
    return square, rest


def body(feats, prior_factor, ridge):
    groups = lax.axis_size("row")
    lanes = lax.axis_size("col")
    cols_here = ridge.shape[0]
    share = cols_here // groups
    col_start = lax.axis_index("col") * cols_here
    form = exchange if (groups, lanes) == (4, 8) else gathered
    square, rest = form(feats, prior_factor, ridge, groups, lanes, share)
    out = chol_solve(square, rest, col_start // NB, lax.axis_index("row"), groups)
    if cols_here < NB:
        out = lax.dynamic_slice_in_dim(out, col_start % NB, cols_here, 1)
    return out


def solution(mesh):
    return jax.shard_map(
        body,
        mesh=mesh,
        in_specs=(P("row", "col"), P("row", "col"), P("col")),
        out_specs=P("row", "col"),
        check_vma=False,
    )
```

```python
import functools
import jax
import jax.numpy as jnp
from jax import lax
from jax.sharding import PartitionSpec as P
from jax.experimental import pallas as pl
from jax.experimental.pallas import tpu as pltpu

NB = 128
PB = 32
TILE = 256
STOPS = (1, 2)


def split2(x):
    hi = x.astype(jnp.bfloat16)
    lo = (x - hi.astype(jnp.float32)).astype(jnp.bfloat16)
    return hi, lo


def dot3(a, b, b_dim=0):
    ah, al = split2(a)
    bh, bl = split2(b)
    return lax.dot_general(
        jnp.concatenate([ah, ah, al], axis=1),
        jnp.concatenate([bh, bl, bh], axis=b_dim),
        (((1,), (b_dim,)), ((), ())),
        preferred_element_type=jnp.float32,
    )


def spread(row, rows=8):
    return jnp.broadcast_to(row, (rows, row.shape[1]))


def factor_block(block):
    sub = lax.broadcasted_iota(jnp.int32, (8, NB), 0)
    sub2 = lax.broadcasted_iota(jnp.int32, (8, 2 * NB), 0)
    lane = lax.broadcasted_iota(jnp.int32, (NB, NB), 1)
    line = lax.broadcasted_iota(jnp.int32, (NB, NB), 0)
    trail = jnp.concatenate([block, (lane == line).astype(jnp.float32)], axis=1)
    nt = PB // 8
    done = []
    for p in range(NB // PB):
        base = p * PB
        panel = trail[:PB]
        rows = [panel[8 * t:8 * t + 8] for t in range(nt)]
        cols = [
            [
                jnp.broadcast_to(rows[t][:, base + j:base + j + 1], (8, NB)) if t >= j // 8 else None
                for t in range(nt)
            ]
            for j in range(PB)
        ]
        outs = [r for r in rows]
        for j in range(PB):
            tj, ij = divmod(j, 8)
            inv = lax.rsqrt(spread(cols[j][tj][ij:ij + 1]))
            col = [cols[j][t] * inv if t >= tj else None for t in range(nt)]
            prow = spread(rows[tj][ij:ij + 1]) * jnp.concatenate([inv, inv], axis=1)
            outs[tj] = jnp.where(sub2 == ij, prow, outs[tj])
            for k in range(j + 1, PB):
                tk, ik = divmod(k, 8)
                piv = spread(col[tk][ik:ik + 1])
                for t in range(tk, nt):
                    cols[k][t] = cols[k][t] - col[t] * piv
            for t in range(tj, nt):
                rows[t] = rows[t] - jnp.concatenate([col[t], col[t]], axis=1) * prow
        out = jnp.concatenate(outs, axis=0)
        done.append(out)
        if p < NB // PB - 1:
            oh, ol = split2(out)
            rhs = jnp.concatenate([oh, ol, oh], axis=0)
            left = jnp.transpose(out[:, :NB])
            lh, ll = split2(left[base + PB:])
            lhs = jnp.concatenate([lh, lh, ll], axis=1)
            prev = trail[PB:]
            trail = prev - jnp.dot(lhs, rhs, preferred_element_type=jnp.float32)
    full = jnp.concatenate(done, axis=0)
    return jnp.where(lane >= line, full[:, :NB], 0.0), full[:, NB:]


def chol_kernel(col_ref, b_hbm, s_hbm, o_ref, m_ref, t_ref, l_ref, r_ref, x_ref, sems):
    n = m_ref.shape[0]
    blocks = n // NB
    own = col_ref[0]
    grp = col_ref[1]
    groups = col_ref.shape[0] - 2
    heads = n // groups
    cb = pltpu.make_async_copy(b_hbm, m_ref, sems.at[0])
    cs = pltpu.make_async_copy(s_hbm, t_ref, sems.at[1])
    cb.start()
    cs.start()
    cb.wait()
    cs.wait()

    def split_rows(v):
        hi, lo = split2(v)
        return jnp.concatenate([hi, lo, hi], axis=0)

    def split_cols(v):
        hi, lo = split2(v)
        return jnp.concatenate([hi, hi, lo], axis=1)

    def step(k, carry, low):
        at = pl.ds(pl.multiple_of(k * NB, NB), NB)
        diag = m_ref[at, at]
        for tile in range(low, n, TILE):
            right = r_ref[:, tile:tile + TILE]
            m_ref[low:tile + TILE, tile:tile + TILE] -= jnp.dot(
                l_ref[low:tile + TILE, :], right, preferred_element_type=jnp.float32
            )
            t_ref[:, tile:tile + TILE] -= jnp.dot(x_ref[...], right, preferred_element_type=jnp.float32)
        u, w = factor_block(diag)
        new = dot3(w, m_ref[at, low:])
        m_ref[at, low:] = new
        m_ref[at, at] = u
        x = dot3(t_ref[:, at], w, 1)
        r_ref[:, low:] = split_rows(new)
        x_ref[...] = split_cols(x)

        @pl.when(k == own)
        def _():
            o_ref[heads:, :] = x
            line = lax.broadcasted_iota(jnp.int32, (NB, n - low), 0) + k * NB
            lane = lax.broadcasted_iota(jnp.int32, (NB, n - low), 1) + low
            mine = jnp.where(lane >= line, m_ref[at, low:], 0.0)
            pick = (
                lax.broadcasted_iota(jnp.int32, (heads, n - low), 1) + low
                == lax.broadcasted_iota(jnp.int32, (heads, n - low), 0) * groups + grp
            ).astype(jnp.bfloat16)
            hi, lo = split2(mine)
            lo2 = (mine - hi.astype(jnp.float32) - lo.astype(jnp.float32)).astype(jnp.bfloat16)
            nt = (((1,), (1,)), ((), ()))
            o_ref[:heads, :] = sum(
                lax.dot_general(pick, v, nt, preferred_element_type=jnp.float32) for v in (hi, lo, lo2)
            )

        @pl.when(k + 1 < blocks)
        def _():
            nxt = pl.ds(pl.multiple_of((k + 1) * NB, NB), NB)
            m_ref[nxt, low:] -= jnp.dot(
                split_cols(jnp.transpose(m_ref[at, nxt])), r_ref[:, low:], preferred_element_type=jnp.float32
            )
            lane = lax.broadcasted_iota(jnp.int32, (NB, n - low), 1) + low
            later = jnp.where(lane >= (k + 2) * NB, new, 0.0)
            l_ref[low:, :] = split_cols(jnp.transpose(later))

        return carry

    r_ref[...] = jnp.zeros_like(r_ref)
    l_ref[...] = jnp.zeros_like(l_ref)
    x_ref[...] = jnp.zeros_like(x_ref)
    first = 0
    for last in STOPS:
        stop = blocks * last // STOPS[-1]
        lax.fori_loop(first, stop, functools.partial(step, low=first * NB), 0)
        first = stop


def chol_solve(square, rest, own, grp, groups):
    n = square.shape[0]
    pos = jnp.stack([own, grp] + [jnp.int32(0)] * groups).astype(jnp.int32)
    return pl.pallas_call(
        chol_kernel,
        out_shape=jax.ShapeDtypeStruct((n // groups + rest.shape[0], NB), jnp.float32),
        in_specs=[
            pl.BlockSpec(memory_space=pltpu.SMEM),
            pl.BlockSpec(memory_space=pl.ANY),
            pl.BlockSpec(memory_space=pl.ANY),
        ],
        out_specs=pl.BlockSpec(memory_space=pltpu.VMEM),
        scratch_shapes=[
            pltpu.VMEM((n, n), jnp.float32),
            pltpu.VMEM(rest.shape, jnp.float32),
            pltpu.VMEM((n, 3 * NB), jnp.bfloat16),
            pltpu.VMEM((3 * NB, n), jnp.bfloat16),
            pltpu.VMEM((rest.shape[0], 3 * NB), jnp.bfloat16),
            pltpu.SemaphoreType.DMA((2,)),
        ],
        compiler_params=pltpu.CompilerParams(vmem_limit_bytes=48 * 1024 * 1024),
    )(pos, square, rest)


EDGES = 4096
MESH = pl.DeviceIdType.MESH


def exchange_kernel(feats_ref, prior_ref, ridge_ref, sq_ref, rs_ref, gf, gp, ff, fp, parts_ref, sendf, recvf,
                    sendp, recvp, got1, acc, got2, send1, recv1, send2, recv2, sends, arrive):
    groups, lanes = sq_ref.shape[:2]
    share, width = sq_ref.shape[2:]
    i = lax.axis_index("row")
    c = lax.axis_index("col")
    core, x, y = lax.rem(c, 2), lax.rem(c // 2, 2), c // 4
    sib = c + 1 - 2 * core
    xn = c + 2 - 4 * x
    yn = c + 4 - 8 * y
    dg = xn + 4 - 8 * y
    planes = [lax.rem(i + d, groups) for d in range(groups)]
    barrier = pltpu.get_barrier_semaphore()
    for col in (sib, xn, yn, dg):
        pl.semaphore_signal(barrier, inc=1, device_id=(i, col), device_id_type=MESH)
    for z in planes[1:]:
        pl.semaphore_signal(barrier, inc=1, device_id=(z, c), device_id_type=MESH)
    pl.semaphore_wait(barrier, 3 + groups)

    def remote(src, dst, s, r, target):
        copy = pltpu.make_async_remote_copy(
            src_ref=src, dst_ref=dst, send_sem=s, recv_sem=r, device_id=target, device_id_type=MESH
        )
        copy.start()
        return copy

    heads = lanes * share
    early = []
    for d, z in enumerate(planes[1:]):
        early.append(remote(feats_ref.at[:heads], gf.at[i], sendf.at[d], recvf.at[i], (z, c)))
    for d, z in enumerate(planes[1:]):
        early.append(remote(prior_ref.at[:heads], gp.at[i], sendp.at[d], recvp.at[i], (z, c)))

    def place(z, value):
        pick = lax.broadcasted_iota(jnp.int32, (width, heads), 0) == (
            lax.broadcasted_iota(jnp.int32, (width, heads), 1) * groups + z
        )
        return jnp.dot(pick.astype(jnp.bfloat16), value, preferred_element_type=jnp.float32)

    def interleave(own_ref, got, to, sem):
        to[...] = place(i, own_ref[:heads, :])
        for z in planes[1:]:
            pltpu.make_async_copy(got.at[z], got.at[z], sem.at[z]).wait()
            to[...] += place(z, got[z])

    nt = (((1,), (1,)), ((), ()))

    def dot_nt(a, b):
        return lax.dot_general(a, b, nt, preferred_element_type=jnp.float32)

    mine = pl.ds(pl.multiple_of(i * heads, heads), heads)
    interleave(feats_ref, gf, ff, recvf)
    wide = ff[...]
    cols = wide.astype(jnp.bfloat16)
    hi, lo = split2(wide * wide)
    ones = jnp.ones((8, wide.shape[1]), jnp.bfloat16)
    col_sq = (dot_nt(ones, hi) + dot_nt(ones, lo))[:1]
    lead = ff[mine, :]
    tail = feats_ref[heads:, :]
    for n, rows in enumerate((lead.astype(jnp.bfloat16), tail)):
        own = rows.astype(jnp.float32)
        dist = jnp.sum(own * own, axis=1, keepdims=True) + col_sq - 2.0 * dot_nt(rows, cols)
        each = rows.shape[0] // lanes
        for k in range(lanes):
            parts_ref[k // 2, k % 2, n * share:n * share + each, :width] = dist[k * each:k * each + each]
    order = [dg // 2, xn // 2, yn // 2, c // 2]
    pair = []
    across = []

    def add_over_pair(h):
        half = pl.ds(h * width, width)
        begun = [
            remote(parts_ref.at[q, 1 - core, :, half], got1.at[4 * h + n], send1.at[4 * h + n],
                   recv1.at[4 * h + n], (i, sib))
            for n, q in enumerate(order)
        ]
        pair.extend(begun)
        for n, q in enumerate(order):
            begun[n].wait_recv()
            acc[4 * h + n] = parts_ref[q, core, :, half] + got1[4 * h + n]
            if n < 3:
                across.append(
                    remote(acc.at[4 * h + n], got2.at[3 * h + n], send2.at[3 * h + n],
                           recv2.at[3 * h + n], (i, (dg, xn, yn)[n]))
                )

    add_over_pair(0)
    interleave(prior_ref, gp, fp, recvp)
    cols = fp[...].astype(jnp.bfloat16)
    line = lax.broadcasted_iota(jnp.int32, (heads, width), 0) + i * heads
    lane = lax.broadcasted_iota(jnp.int32, (heads, width), 1)
    first = c * (width // lanes)
    here = (lane == line) & (lane >= first) & (lane < first + width // lanes)
    ridge = jnp.where(here, jnp.concatenate([ridge_ref[...]] * lanes, axis=1), 0.0)
    for n, rows in enumerate((fp[mine, :].astype(jnp.bfloat16), prior_ref[heads:, :])):
        update = dot_nt(rows, cols)
        if n == 0:
            update = update - ridge
        each = rows.shape[0] // lanes
        for k in range(lanes):
            parts_ref[k // 2, k % 2, n * share:n * share + each, width:] = update[k * each:k * each + each]

    add_over_pair(1)
    for copy in across:
        copy.wait_recv()
    dist, update = [acc[4 * h + 3] + got2[3 * h] + got2[3 * h + 1] + got2[3 * h + 2] for h in range(2)]
    system = jnp.exp(-dist / EDGES) - update
    sq_ref[i, c] = system[:share]
    rs_ref[c] = system[share:]

    started = []

    def pass_on(z, col, target):
        n = len(started)
        started.append(
            remote(sq_ref.at[z, col], sq_ref.at[z, col], sends.at[n], arrive.at[z * lanes + col], target)
        )

    def pass_rest(col, target):
        n = len(started)
        started.append(
            remote(rs_ref.at[col], rs_ref.at[col], sends.at[n], arrive.at[groups * lanes + col], target)
        )

    def await_block(z, col):
        pltpu.make_async_copy(sq_ref.at[z, col], sq_ref.at[z, col], arrive.at[z * lanes + col]).wait()

    def await_rest(col):
        pltpu.make_async_copy(rs_ref.at[col], rs_ref.at[col], arrive.at[groups * lanes + col]).wait()

    for z in planes[1:]:
        pass_on(i, c, (z, c))
    for z in planes:
        if z is not planes[0]:
            await_block(z, c)
        pass_on(z, c, (i, xn))
        pass_on(z, c, (i, yn))
        pass_on(z, c, (i, sib))
        if z is planes[0]:
            for col in (xn, yn, sib):
                pass_rest(c, (i, col))
    for n, z in enumerate(planes):
        await_block(z, xn)
        if n < groups // 2:
            pass_on(z, xn, (i, yn))
        pass_on(z, xn, (i, sib))
        await_block(z, yn)
        if n >= groups // 2:
            pass_on(z, yn, (i, xn))
        pass_on(z, yn, (i, sib))
        if n == 0:
            await_rest(xn)
            pass_rest(xn, (i, yn))
            pass_rest(xn, (i, sib))
            await_rest(yn)
            pass_rest(yn, (i, sib))
    for n, z in enumerate(planes):
        await_block(z, dg)
        pass_on(z, dg, (i, sib))
        if n == 0:
            await_rest(dg)
            pass_rest(dg, (i, sib))
    other = [sib + d for d in (0, xn - c, yn - c, dg - c)]
    for col in other:
        for z in planes:
            await_block(z, col)
        await_rest(col)
    for copy in early + pair + across + started:
        copy.wait_send()


def exchange(feats, prior, ridge, groups, lanes, share):
    width = ridge.shape[0] * lanes
    each = feats.shape[0] // lanes
    heads = lanes * share
    wide = 2 * width
    f32 = jnp.float32
    dma = pltpu.SemaphoreType.DMA
    vmem = pl.BlockSpec(memory_space=pltpu.VMEM)
    square, rest = pl.pallas_call(
        exchange_kernel,
        out_shape=(
            jax.ShapeDtypeStruct((groups, lanes, share, width), f32),
            jax.ShapeDtypeStruct((lanes, each - share, width), f32),
        ),
        in_specs=[vmem, vmem, vmem],
        out_specs=(vmem, vmem),
        scratch_shapes=[
            pltpu.VMEM((groups, heads, feats.shape[1]), feats.dtype),
            pltpu.VMEM((groups, heads, prior.shape[1]), prior.dtype),
            pltpu.VMEM((width, feats.shape[1]), f32),
            pltpu.VMEM((width, prior.shape[1]), f32),
            pltpu.VMEM((lanes // 2, 2, each, wide), f32),
            dma((groups - 1,)),
            dma((groups,)),
            dma((groups - 1,)),
            dma((groups,)),
            pltpu.VMEM((8, each, width), f32),
            pltpu.VMEM((8, each, width), f32),
            pltpu.VMEM((6, each, width), f32),
            dma((8,)),
            dma((8,)),
            dma((6,)),
            dma((6,)),
            dma((64,)),
            dma((groups * lanes + lanes,)),
        ],
        compiler_params=pltpu.CompilerParams(
            collective_id=1, has_side_effects=True, vmem_limit_bytes=56 * 1024 * 1024
        ),
    )(feats, prior, ridge[None, :])
    return square.reshape(-1, width), rest.reshape(-1, width)

def subject_rows(parts, groups, count):
    width = parts.shape[-1]
    return parts.reshape(groups, count, width).transpose(1, 0, 2).reshape(groups * count, width)


def dealt(head, tail, lanes):
    width = head.shape[1]
    both = [head.reshape(lanes, -1, width), tail.reshape(lanes, -1, width)]
    return jnp.concatenate(both, axis=1).reshape(-1, width)


def gathered(feats, prior_factor, ridge, groups, lanes, share):
    row_pos = lax.axis_index("row")
    col_pos = lax.axis_index("col")
    cols_here = ridge.shape[0]
    total_cols = cols_here * lanes
    leading = share * lanes
    col_feats, col_prior = (
        lax.all_gather(feats[:leading], "row", axis=0, tiled=True),
        lax.all_gather(prior_factor[:leading], "row", axis=0, tiled=True),
    )
    col_feats = subject_rows(col_feats, groups, leading)
    col_prior = subject_rows(col_prior, groups, leading)
    first = row_pos * leading
    rows_feats = dealt(lax.dynamic_slice_in_dim(col_feats, first, leading), feats[leading:], lanes)
    rows_prior = dealt(lax.dynamic_slice_in_dim(col_prior, first, leading), prior_factor[leading:], lanes)
    subject = dealt(
        first + lax.broadcasted_iota(jnp.int32, (leading, 1), 0),
        jnp.full((feats.shape[0] - leading, 1), -1, jnp.int32),
        lanes,
    )
    col_start = col_pos * cols_here
    column = lax.broadcasted_iota(jnp.int32, (1, total_cols), 1)
    own_ridge = lax.dynamic_update_slice(jnp.zeros((total_cols,), jnp.float32), ridge, (col_start,))
    wide_rows = rows_feats.astype(jnp.float32)
    wide_cols = col_feats.astype(jnp.float32)
    gram = jnp.dot(rows_feats, col_feats.T, preferred_element_type=jnp.float32)
    dist = (
        jnp.sum(wide_rows * wide_rows, axis=1)[:, None]
        + jnp.sum(wide_cols * wide_cols, axis=1)[None, :]
        - 2.0 * gram
    )
    update = jnp.dot(rows_prior, col_prior.T, preferred_element_type=jnp.float32)
    update = update - jnp.where(subject == column, own_ridge[None, :], 0.0)
    sums = lax.psum_scatter(
        jnp.concatenate([dist, update], axis=1), "col", scatter_dimension=0, tiled=True
    )
    system = jnp.exp(-sums[:, :total_cols] / EDGES) - sums[:, total_cols:]
    square = lax.all_gather(system[:share], ("row", "col"), axis=0, tiled=True)
    rest = lax.all_gather(system[share:], "col", axis=0, tiled=True)
    return square, rest


def body(feats, prior_factor, ridge):
    groups = lax.axis_size("row")
    lanes = lax.axis_size("col")
    cols_here = ridge.shape[0]
    share = cols_here // groups
    col_start = lax.axis_index("col") * cols_here
    form = exchange if (groups, lanes) == (4, 8) else gathered
    square, rest = form(feats, prior_factor, ridge, groups, lanes, share)
    out = chol_solve(square, rest, col_start // NB, lax.axis_index("row"), groups)
    if cols_here < NB:
        out = lax.dynamic_slice_in_dim(out, col_start % NB, cols_here, 1)
    return out


def solution(mesh):
    return jax.shard_map(
        body,
        mesh=mesh,
        in_specs=(P("row", "col"), P("row", "col"), P("col")),
        out_specs=P("row", "col"),
        check_vma=False,
    )
```
